256 devices in a mesh: cores: 4 (over x), mode: 64 (over z, y, core).
Axes of the slice: x: 4, y: 4, z: 8, core: 2. Of those that a mesh axis runs over, the one named last changes fastest.
Arguments:
- x_cores: bfloat16 [4, 512, 1024, 512], P('cores', None, 'mode'), may hold values from -0.25 to 0.25
- y_cores: bfloat16 [4, 256, 1024, 256], P('cores', None, 'mode'), may hold values from -40 to 40
- left_boundary: bfloat16 [256, 512], replicated, may hold values from -6 to 6
- right_boundary: bfloat16 [256, 512], replicated, may hold values from -6 to 6
Outputs:
- projected: bfloat16 [4, 256, 1024, 256], P('cores', None, 'mode')
The draws below stay inside these ranges and needn't reach their ends.
All inputs are finite; a program needn't handle non-finite values.
Results may differ from the reference program's by a relative error of at most 0.014.
Values may be sent and summed in bfloat16 or wider, within the bound.
No kernel may reach another device: no remote copies, remote signals or barrier semaphores. Data moves between devices by JAX's collectives and lax.ppermute only.
A program may use at most 128 MiB of HBM per device.

```python
import math
import jax
import jax.numpy as jnp
from jax import lax

RANK_X = 512
RANK_Y = 256
NCORES = 4
MODES = 1024


def draw_y_cores(key, part):
    base_key = jax.random.fold_in(key, 17)
    first_key, second_key, third_key = jax.random.split(base_key, 3)
    shape_full = (NCORES, RANK_Y, MODES, RANK_Y)
    left_scale = jnp.exp(jax.random.uniform(first_key, (NCORES, RANK_Y, 1, 1)) * math.log(10.0))
    right_scale = jnp.exp(jax.random.uniform(second_key, (NCORES, 1, 1, RANK_Y)) * math.log(10.0))
    sampled = jax.random.normal(third_key, shape_full)
    values = jnp.clip(sampled * left_scale * right_scale / math.sqrt(RANK_Y), -40.0, 40.0)
    return values.astype(jnp.bfloat16)


def shard_levels(key, shape, pieces, least, high):
    factor_of = 1.0
    for axis_at, blocks in pieces:
        steps = jax.random.uniform(jax.random.fold_in(jax.random.fold_in(key, 6), axis_at), (blocks,), jnp.float32, least / len(pieces), high / len(pieces))
        factor_of = factor_of * jnp.repeat(jnp.exp(steps), shape[axis_at] // blocks).reshape((-1,) + (1,) * (len(shape) - 1 - axis_at))
    return factor_of


def noise(stream_key, dims, width, bound, cuts=(), kind=jnp.bfloat16):
    factor_of = shard_levels(stream_key, dims, cuts, -0.22, 0.18) if cuts else 1.0
    entries = jax.random.normal(stream_key, dims, jnp.float32) * width * factor_of
    return jnp.minimum(jnp.maximum(entries, -bound), bound).astype(kind)


def setup_inputs(seed: int = 0) -> dict:
    key_of = jax.random.split(jax.random.key(seed), 5)
    return {
        "x_cores": noise(key_of[0], (NCORES, RANK_X, MODES, RANK_X), RANK_X ** -0.5, 0.25, ((0, 4), (2, 64))),
        "y_cores": draw_y_cores(jax.random.fold_in(key_of[4], 71), 0),
        "left_boundary": noise(key_of[2], (RANK_Y, RANK_X), 1.0, 6.0),
        "right_boundary": noise(key_of[3], (RANK_Y, RANK_X), 1.0, 6.0),
    }


epsilon = 1e-06

def normalized(summed):
    return (summed * lax.rsqrt(jnp.mean(summed * summed) + epsilon)).astype(jnp.bfloat16)

def reference(x_cores, y_cores, left_boundary, right_boundary):
    core_count = x_cores.shape[0]
    environ = left_boundary
    applied_list = []
    for core_index in range(core_count):
        source = x_cores[core_index]
        target = y_cores[core_index]
        applied = jnp.dot(environ, source.reshape(RANK_X, MODES * RANK_X), preferred_element_type=jnp.float32).astype(jnp.bfloat16)
        applied_list.append(applied)
        if core_index < core_count - 1:
            summed = lax.dot_general(target.reshape(RANK_Y * MODES, RANK_Y), applied.reshape(RANK_Y * MODES, RANK_X), (((0,), (0,)), ((), ())), preferred_element_type=jnp.float32)
            environ = normalized(summed)
    environ = right_boundary
    results = [None] * core_count
    for core_index in reversed(range(core_count)):
        applied = applied_list[core_index].reshape(RANK_Y * MODES, RANK_X)
        product = lax.dot_general(applied, environ, (((1,), (1,)), ((), ())), preferred_element_type=jnp.float32) * (1.0 / math.sqrt(RANK_X))
        results[core_index] = product.astype(jnp.bfloat16).reshape(RANK_Y, MODES, RANK_Y)
        if core_index > 0:
            source = x_cores[core_index]
            target = y_cores[core_index]
            carried_back = lax.dot_general(source.reshape(RANK_X * MODES, RANK_X), environ, (((1,), (1,)), ((), ())), preferred_element_type=jnp.float32).astype(jnp.bfloat16)
            carried_back = carried_back.reshape(RANK_X, MODES * RANK_Y)
            summed = lax.dot_general(target.reshape(RANK_Y, MODES * RANK_Y), carried_back, (((1,), (1,)), ((), ())), preferred_element_type=jnp.float32)
            environ = normalized(summed)
    return jnp.stack(results)
```

```python
import functools
import math

import jax
import jax.numpy as jnp
from jax import lax
from jax.experimental import pallas as pl
from jax.experimental.pallas import tpu as pltpu
from jax.sharding import PartitionSpec as P

EPSILON = 1e-06
TILES = 8
VMEM_LIMIT = 56 * 1024 * 1024
BF16 = jnp.bfloat16
F32 = jnp.float32
NT = (((1,), (1,)), ((), ()))
TN = (((0,), (0,)), ((), ()))


def dims_of(x, y):
    source_rank, points = x.shape[0], x.shape[1]
    return y.shape[0], source_rank, points


def unpack(e_ref, env_ref):
    chunks, rows, width = e_ref.shape
    lanes = env_ref.shape[1] // width
    for j in range(chunks):
        r, k = j // lanes, j % lanes
        env_ref[rows * r : rows * (r + 1), width * k : width * (k + 1)] = e_ref[j]


def pack(value, s_ref):
    chunks, rows, width = s_ref.shape
    lanes = value.shape[1] // width
    for j in range(chunks):
        r, k = j // lanes, j % lanes
        s_ref[j] = value[rows * r : rows * (r + 1), width * k : width * (k + 1)]


def scale_of(env):
    wide = env.astype(F32)
    return lax.rsqrt(jnp.mean(wide * wide) + EPSILON)


def load_tiles(x_ref, x_buf, sems):
    rows = x_buf.shape[0] // TILES
    copies = []
    for t in range(TILES):
        part = pl.ds(t * rows, rows)
        copies.append(pltpu.make_async_copy(x_ref.at[part], x_buf.at[part], sems.at[t]))
    for copy in copies:
        copy.start()
    return copies


def halves(width):
    return [slice(start, start + 128) for start in range(0, width, 128)]


def mode_major(y_buf, wide, y2_buf, points):
    rows, width = y2_buf.shape[0], y_buf.shape[1]
    for h, part in enumerate(halves(width)):
        wide[h, 0 : rows * points, :] = y_buf[:, part].astype(F32)
        for i in range(points):
            y2_buf[:, i * width + part.start : i * width + part.stop] = wide[
                h, pl.ds(i, rows, stride=points), :
            ].astype(BF16)


def left_sum(env, scale, x_buf, copies, y2_buf, wide, points):
    width = y2_buf.shape[1] // points
    source_rank = env.shape[1]
    turned = env.T
    for i in range(points):
        w = jnp.dot(turned, y2_buf[:, i * width : (i + 1) * width], preferred_element_type=F32)
        w = w * scale
        for h, part in enumerate(halves(width)):
            wide[h, pl.ds(i, source_rank, stride=points), :] = w[:, part]
    rows = x_buf.shape[0] // TILES
    total = None
    for t in range(TILES):
        part = pl.ds(t * rows, rows)
        copies[t].wait()
        w = jnp.concatenate([wide[h, part, :] for h in range(wide.shape[0])], axis=1).astype(BF16)
        term = lax.dot_general(w, x_buf[part, :], TN, preferred_element_type=F32)
        total = term if total is None else total + term
    return total


def carry_back(env, scale, x_buf, copies, wide, cb_buf, points):
    rows = x_buf.shape[0] // TILES
    width = env.shape[0]
    ranks = rows // points
    for t in range(TILES):
        part = pl.ds(t * rows, rows)
        copies[t].wait()
        value = lax.dot_general(x_buf[part, :], env, NT, preferred_element_type=F32) * scale
        for h, lanes in enumerate(halves(width)):
            wide[h, part, :] = value[:, lanes]
        for h, lanes in enumerate(halves(width)):
            for i in range(points):
                cb_buf[
                    t * ranks : (t + 1) * ranks, i * width + lanes.start : i * width + lanes.stop
                ] = wide[h, pl.ds(t * rows + i, ranks, stride=points), :].astype(BF16)


def first_kernel(points, role, lb, rb, x, y, s, cb, y2, x_buf, y_buf, y2_buf, cb_buf, wide, sems, side):
    load_y = pltpu.make_async_copy(y, y_buf, side.at[0])
    load_y.start()

    def prepare():
        load_y.wait()
        mode_major(y_buf, wide, y2_buf, points)
        store = pltpu.make_async_copy(y2_buf, y2, side.at[1])
        store.start()
        return store

    @pl.when(role[0] == 1)
    def _():
        copies = load_tiles(x, x_buf, sems)
        store = prepare()
        pack(left_sum(lb[...], 1.0, x_buf, copies, y2_buf, wide, points).astype(BF16), s)
        store.wait()

    @pl.when(role[0] == 2)
    def _():
        copies = load_tiles(x, x_buf, sems)
        store = prepare()
        carry_back(rb[...], 1.0, x_buf, copies, wide, cb_buf, points)
        keep = pltpu.make_async_copy(cb_buf, cb, side.at[0])
        keep.start()
        total = lax.dot_general(y2_buf[...], cb_buf[...], NT, preferred_element_type=F32)
        pack(total.astype(BF16), s)
        keep.wait()
        store.wait()

    @pl.when(role[0] == 0)
    def _():
        store = prepare()
        s[...] = jnp.zeros_like(s)
        store.wait()


def next_kernel(points, role, e, x, y2, cb_in, s, cb, x_buf, y2_buf, cb_buf, wide, env_buf, sems, side):
    del cb_in

    def begin():
        load_y = pltpu.make_async_copy(y2, y2_buf, side.at[0])
        load_y.start()
        copies = load_tiles(x, x_buf, sems)
        unpack(e, env_buf)
        return load_y, copies

    @pl.when(role[0] == 1)
    def _():
        load_y, copies = begin()
        env = env_buf[...]
        scale = scale_of(env)
        load_y.wait()
        pack(left_sum(env, scale, x_buf, copies, y2_buf, wide, points).astype(BF16), s)

    @pl.when(role[0] == 2)
    def _():
        load_y, copies = begin()
        env = env_buf[...]
        scale = scale_of(env)
        carry_back(env, scale, x_buf, copies, wide, cb_buf, points)
        load_y.wait()
        keep = pltpu.make_async_copy(cb_buf, cb, side.at[0])
        keep.start()
        total = lax.dot_general(y2_buf[...], cb_buf[...], NT, preferred_element_type=F32)
        pack(total.astype(BF16), s)
        keep.wait()

    @pl.when(role[0] == 0)
    def _():
        s[...] = jnp.zeros_like(s)


def last_kernel(points, group, lb, e1, e2, e3, x, cb, out, x_buf, cb_buf, wide, env_buf, renv_buf, sems, side):
    target_rank, source_rank = lb.shape
    width = target_rank
    norm = 1.0 / math.sqrt(source_rank)

    def project(env, scale):
        for i in range(points):
            value = jnp.dot(env, cb_buf[:, i * width : (i + 1) * width], preferred_element_type=F32)
            value = value * (scale * norm)
            for h, lanes in enumerate(halves(width)):
                wide[h, pl.ds(i, target_rank, stride=points), :] = value[:, lanes]
        for h, lanes in enumerate(halves(width)):
            out[:, lanes] = wide[h, 0 : target_rank * points, :].astype(BF16)

    @pl.when(group[0] == 0)
    def _():
        copies = load_tiles(x, x_buf, sems)
        unpack(e3, renv_buf)
        renv = renv_buf[...]
        carry_back(renv, scale_of(renv), x_buf, copies, wide, cb_buf, points)
        project(lb[...], 1.0)

    @pl.when(group[0] != 0)
    def _():
        load = pltpu.make_async_copy(cb, cb_buf, side.at[0])
        load.start()

        @pl.when(group[0] == 1)
        def _():
            unpack(e1, env_buf)

        @pl.when(group[0] == 2)
        def _():
            unpack(e2, env_buf)

        @pl.when(group[0] == 3)
        def _():
            unpack(e3, env_buf)

        env = env_buf[...]
        scale = scale_of(env)
        load.wait()
        project(env, scale)


def place(kind):
    return pl.BlockSpec(memory_space=kind)


SMEM, VMEM, ANY = pltpu.SMEM, pltpu.VMEM, pl.ANY


def exchange(partial_sum, route):
    chunks, rows, width = partial_sum.shape
    devices = lax.axis_size("mode")
    chips = devices // 2
    core = lax.axis_index("mode") % 2
    same_core = [list(range(c, devices, 2)) for c in range(2)]
    same_chip = [[d, d + 1] for d in range(0, devices, 2)]
    half = partial_sum.reshape(2, chunks // 2, rows, width)
    kept = lax.dynamic_index_in_dim(half, core, 0, keepdims=False)
    given = lax.dynamic_index_in_dim(half, 1 - core, 0, keepdims=False)
    taken = lax.ppermute(given, "mode", [(d, d ^ 1) for d in range(devices)])
    chip = (kept.astype(F32) + taken.astype(F32)).astype(BF16)
    mine = lax.all_to_all(chip, "mode", 0, 0, axis_index_groups=same_core, tiled=True)
    share = chunks // devices
    mine = mine.reshape(chips, share * rows, width)
    summed = jnp.sum(mine.astype(F32), axis=0).astype(BF16)
    summed = lax.ppermute(summed, "cores", route)
    spread = jnp.broadcast_to(summed[None], (chips, share * rows, width))
    whole = lax.all_to_all(spread, "mode", 0, 0, axis_index_groups=same_core, tiled=True)
    whole = lax.all_gather(whole, "mode", axis_index_groups=same_chip)
    return whole.reshape(chunks, rows, width)


def body(x_cores, y_cores, left_boundary, right_boundary):
    _, source_rank, points, _ = x_cores.shape
    target_rank = left_boundary.shape[0]
    group = lax.axis_index("cores")
    x = x_cores.reshape(source_rank * points, source_rank)
    y = y_cores.reshape(target_rank * points, target_rank)
    chunk = (64, target_rank * source_rank // (64 * 128), 128)
    rows = source_rank * points
    flat = points * target_rank
    s_shape = jax.ShapeDtypeStruct(chunk, BF16)
    cb_shape = jax.ShapeDtypeStruct((source_rank, flat), BF16)
    y2_shape = jax.ShapeDtypeStruct((target_rank, flat), BF16)
    x_buf = pltpu.VMEM((rows, source_rank), BF16)
    y2_buf = pltpu.VMEM((target_rank, flat), BF16)
    cb_buf = pltpu.VMEM((source_rank, flat), BF16)
    wide = pltpu.VMEM((target_rank // 128, rows, 128), F32)
    env_buf = pltpu.VMEM((target_rank, source_rank), BF16)
    sems = pltpu.SemaphoreType.DMA((TILES,))
    side = pltpu.SemaphoreType.DMA((2,))
    params = pltpu.CompilerParams(vmem_limit_bytes=VMEM_LIMIT)

    def role_at(position):
        left = group == position
        right = group == 3 - position
        return jnp.where(left, 1, jnp.where(right, 2, 0)).astype(jnp.int32).reshape(1)

    summed, cb, y2 = pl.pallas_call(
        functools.partial(first_kernel, points),
        out_shape=(s_shape, cb_shape, y2_shape),
        in_specs=[place(SMEM), place(VMEM), place(VMEM), place(ANY), place(ANY)],
        out_specs=(place(VMEM), place(ANY), place(ANY)),
        scratch_shapes=[
            x_buf, pltpu.VMEM((target_rank * points, target_rank), BF16), y2_buf, cb_buf, wide, sems, side,
        ],
        compiler_params=params,
        name="first_step",
    )(role_at(0), left_boundary, right_boundary, x, y)

    envs = [exchange(summed, [(0, 1), (3, 2)])]
    for position, route in ((1, [(1, 2), (2, 1)]), (2, [(2, 3), (1, 0)])):
        summed, cb = pl.pallas_call(
            functools.partial(next_kernel, points),
            out_shape=(s_shape, cb_shape),
            in_specs=[place(SMEM), place(VMEM), place(ANY), place(ANY), place(ANY)],
            out_specs=(place(VMEM), place(ANY)),
            scratch_shapes=[x_buf, y2_buf, cb_buf, wide, env_buf, sems, side],
            input_output_aliases={4: 1},
            compiler_params=params,
            name="next_step",
        )(role_at(position), envs[-1], x, y2, cb)
        envs.append(exchange(summed, route))

    out = pl.pallas_call(
        functools.partial(last_kernel, points),
        out_shape=jax.ShapeDtypeStruct((target_rank * points, target_rank), BF16),
        in_specs=[place(SMEM)] + [place(VMEM)] * 4 + [place(ANY)] * 2,
        out_specs=place(VMEM),
        scratch_shapes=[x_buf, cb_buf, wide, env_buf, env_buf, sems, side],
        compiler_params=params,
        name="projection",
    )(group.astype(jnp.int32).reshape(1), left_boundary, *envs, x, cb)
    return out.reshape(1, target_rank, points, target_rank)


def solution(mesh):
    in_specs = (P("cores", None, "mode", None), P("cores", None, "mode", None), P(), P())
    out_specs = P("cores", None, "mode", None)
    return jax.shard_map(body, mesh=mesh, in_specs=in_specs, out_specs=out_specs, check_vma=False)
```

```python
import functools
import math

import jax
import jax.numpy as jnp
from jax import lax
from jax.experimental import pallas as pl
from jax.experimental.pallas import tpu as pltpu
from jax.sharding import PartitionSpec as P

EPSILON = 1e-06
TILES = 8
PARTS = 4
WINDOW = 3
LANES = 128
VMEM_LIMIT = 36 * 1024 * 1024
BF16 = jnp.bfloat16
F32 = jnp.float32
NT = (((1,), (1,)), ((), ()))
TN = (((0,), (0,)), ((), ()))
SMEM, VMEM, HBM = pltpu.SMEM, pltpu.VMEM, pltpu.HBM
IDLE, LEFT, RIGHT, APPLY = 0, 1, 2, 3


def unpack(e_ref, env_ref):
    chunks, rows, width = e_ref.shape
    lanes = env_ref.shape[1] // width
    for j in range(chunks):
        r, k = j // lanes, j % lanes
        env_ref[rows * r : rows * (r + 1), width * k : width * (k + 1)] = e_ref[j]


def hand_out(acc, scale, core, kept, given):
    chunks, rows, width = kept.shape
    lanes = acc.shape[1] // width
    half = acc.shape[0] // 2
    for ref, owner in ((given, 1 - core), (kept, core)):
        start = pl.multiple_of(owner * half, half)
        for j in range(chunks):
            r, k = j // lanes, j % lanes
            value = acc[pl.ds(start + rows * r, rows), width * k : width * (k + 1)]
            if scale is not None:
                value = value * scale
            ref[j] = value.astype(BF16)


def scale_of(env):
    wide = env.astype(F32)
    return lax.rsqrt(jnp.mean(wide * wide) + EPSILON)


def tile_copies(x_ref, x_buf, sems):
    rows = x_buf.shape[0] // TILES
    parts = [pl.ds(t * rows, rows) for t in range(TILES)]
    return [pltpu.make_async_copy(x_ref.at[p], x_buf.at[p], sems.at[t]) for t, p in enumerate(parts)]


def begin(copies, count):
    for copy in copies[:count]:
        copy.start()


def arrive(copies, t):
    copies[t].wait()
    if t + WINDOW < len(copies):
        copies[t + WINDOW].start()


def mode_major(y_buf, y2, points):
    step = y2.shape[0] // 8
    for t in range(8):
        part = y_buf[t * step * points : (t + 1) * step * points, :]
        y2[t * step : (t + 1) * step, :] = part.reshape(step, y2.shape[1])


def left_sum(env, x, copies, y2, w, acc):
    width = env.shape[0]
    turned = env.T
    for i in range(y2.shape[1] // width):
        lanes = slice(i * width, (i + 1) * width)
        w[:, lanes] = jnp.dot(turned, y2[:, lanes], preferred_element_type=F32).astype(BF16)
    rows = x.shape[0] // PARTS
    ranks = w.shape[0] // PARTS
    total = None
    for t in range(PARTS):
        for tile in range(t * (TILES // PARTS), (t + 1) * (TILES // PARTS)):
            copies[tile].wait()
        own = w[t * ranks : (t + 1) * ranks, :].reshape(rows, width)
        term = lax.dot_general(own, x[t * rows : (t + 1) * rows, :], TN, preferred_element_type=F32)
        total = term if total is None else total + term
    acc[...] = total


def carry_back(env, x, copies, natural, cb, stores):
    rows = x.shape[0] // TILES
    ranks = cb.shape[0] // TILES
    turned = env.T
    for t in range(TILES):
        arrive(copies, t)
        value = jnp.dot(x[t * rows : (t + 1) * rows, :], turned, preferred_element_type=F32)
        natural[t * rows : (t + 1) * rows, :] = value.astype(BF16)
        part = natural[t * rows : (t + 1) * rows, :]
        cb[t * ranks : (t + 1) * ranks, :] = part.reshape(ranks, cb.shape[1])
    for store in stores:
        store.start()


def right_sum(y2, cb, acc):
    acc[...] = lax.dot_general(y2[...], cb[...], NT, preferred_element_type=F32)


def apply(env, x, copies, xt, narrow, applied):
    source_rank = env.shape[1]
    rows = x.shape[0] // TILES
    ranks = xt.shape[0] // TILES
    for t in range(TILES):
        arrive(copies, t)
        xt[t * ranks : (t + 1) * ranks, :] = x[t * rows : (t + 1) * rows, :].reshape(ranks, xt.shape[1])
    for i in range(xt.shape[1] // source_rank):
        lanes = slice(i * source_rank, (i + 1) * source_rank)
        narrow[:, lanes] = jnp.dot(env, xt[:, lanes], preferred_element_type=F32).astype(BF16)
    blocks = applied.shape[1] // source_rank
    own = env.shape[0] // blocks
    for j in range(blocks):
        applied[:, j * source_rank : (j + 1) * source_rank] = narrow[
            j * own : (j + 1) * own, :
        ].reshape(source_rank, source_rank)


def first_kernel(
    points, role, lb, rb, x, y, kept, given, cb_out, y2, x_buf, y_buf, cb, w, natural, acc, env_buf, sems, store_sems, side
):
    load_y = pltpu.make_async_copy(y, y_buf, side.at[0])
    stores = tile_copies(cb, cb_out, store_sems)
    copies = tile_copies(x, x_buf, sems)

    @pl.when(role[0] == IDLE)
    def _():
        load_y.start()
        load_y.wait()
        mode_major(y_buf, y2, points)
        kept[...] = jnp.zeros_like(kept)
        given[...] = jnp.zeros_like(given)

    @pl.when(role[0] == LEFT)
    def _():
        load_y.start()
        load_env = pltpu.make_async_copy(lb, env_buf, side.at[2])
        load_env.start()
        load_y.wait()
        begin(copies, TILES)
        mode_major(y_buf, y2, points)
        load_env.wait()
        left_sum(env_buf[...], x_buf, copies, y2, w, acc)
        hand_out(acc, None, role[1], kept, given)

    @pl.when(role[0] == RIGHT)
    def _():
        load_env = pltpu.make_async_copy(rb, env_buf, side.at[2])
        load_env.start()
        load_y.start()
        begin(copies, WINDOW)
        load_env.wait()
        carry_back(env_buf[...], x_buf, copies, natural, cb, stores)
        load_y.wait()
        mode_major(y_buf, y2, points)
        right_sum(y2, cb, acc)
        hand_out(acc, None, role[1], kept, given)
        for store in stores:
            store.wait()


def next_kernel(
    role, e, lb, x, y2, kept, given, cb_out, x_buf, cb, w, natural, xt, narrow, acc, env_buf, sems, store_sems, side
):
    stores = tile_copies(cb, cb_out, store_sems)
    copies = tile_copies(x, x_buf, sems)

    @pl.when(role[0] == IDLE)
    def _():
        kept[...] = jnp.zeros_like(kept)
        given[...] = jnp.zeros_like(given)

    @pl.when(role[0] == APPLY)
    def _():
        kept[...] = jnp.zeros_like(kept)
        given[...] = jnp.zeros_like(given)
        load_env = pltpu.make_async_copy(lb, env_buf, side.at[0])
        load_env.start()
        begin(copies, WINDOW)
        load_env.wait()
        apply(env_buf[...], x_buf, copies, xt, narrow, cb)
        for store in stores:
            store.start()
        for store in stores:
            store.wait()

    @pl.when(role[0] == LEFT)
    def _():
        begin(copies, TILES)
        unpack(e, env_buf)
        env = env_buf[...]
        left_sum(env, x_buf, copies, y2, w, acc)
        hand_out(acc, scale_of(env), role[1], kept, given)

    @pl.when(role[0] == RIGHT)
    def _():
        begin(copies, WINDOW)
        unpack(e, env_buf)
        env = env_buf[...]
        carry_back(env, x_buf, copies, natural, cb, stores)
        right_sum(y2, cb, acc)
        hand_out(acc, scale_of(env), role[1], kept, given)
        for store in stores:
            store.wait()


def last_kernel(points, role, e1, e2, e3, cb0, cb1, cb2, out, cb, out_buf, narrow, env_buf, sems, side):
    target_rank, source_rank = env_buf.shape
    width = target_rank
    norm = 1.0 / math.sqrt(source_rank)
    block = out_buf.shape[0] // TILES
    parts = [pl.ds(t * block, block) for t in range(TILES)]
    stores = [pltpu.make_async_copy(out_buf.at[p], out.at[p], sems.at[t]) for t, p in enumerate(parts)]

    def load(source):
        lanes = [pl.ds(j * source_rank, source_rank) for j in range(cb.shape[1] // source_rank)]
        loads = [
            pltpu.make_async_copy(source.at[:, k], cb.at[:, k], side.at[j]) for j, k in enumerate(lanes)
        ]
        for copy in loads:
            copy.start()
        return loads

    def project(e, source, other):
        loads = load(source)
        unpack(e, env_buf)
        env = env_buf[...]
        factor = scale_of(env) * norm
        if other is not None:
            factor = factor * scale_of(other[...])
        for i in range(points):
            if i * width % source_rank == 0:
                loads[i * width // source_rank].wait()
            part = cb[:, i * width : (i + 1) * width]
            value = jnp.dot(env, part, preferred_element_type=F32) * factor
            narrow[:, i * width : (i + 1) * width] = value.astype(BF16)
        own = target_rank // TILES
        for t in range(TILES):
            out_buf[parts[t], :] = narrow[t * own : (t + 1) * own, :].reshape(block, width)
            stores[t].start()

    @pl.when(role[0] == 0)
    def _():
        loads = load(cb1)
        unpack(e3, env_buf)
        env = env_buf[...]
        factor = scale_of(env) * norm
        for t in range(TILES):
            loads[t].wait()
            value = lax.dot_general(
                cb[:, t * source_rank : (t + 1) * source_rank], env, NT, preferred_element_type=F32)
            out_buf[parts[t], :] = (value * factor).astype(BF16)
            stores[t].start()

    @pl.when(role[0] == 1)
    def _():
        project(e1, cb2, e2)

    @pl.when(role[0] == 2)
    def _():
        project(e2, cb1, e1)

    @pl.when(role[0] == 3)
    def _():
        project(e3, cb0, None)

    for store in stores:
        store.wait()


def place(kind):
    return pl.BlockSpec(memory_space=kind)


def in_hbm(array):
    return pltpu.with_memory_space_constraint(array, HBM)


def step_calls(points, target_rank, source_rank):
    chunk = (32, target_rank * source_rank // (64 * LANES), LANES)
    rows = source_rank * points
    flat = points * target_rank
    s_shape = jax.ShapeDtypeStruct(chunk, BF16)
    cb_shape = jax.ShapeDtypeStruct((source_rank, flat), BF16)
    y2_shape = jax.ShapeDtypeStruct((target_rank, flat), BF16)
    x_buf = pltpu.VMEM((rows, source_rank), BF16)
    cb = pltpu.VMEM(cb_shape.shape, BF16)
    y_buf = pltpu.VMEM((target_rank * points, target_rank), BF16)
    w = pltpu.VMEM(cb_shape.shape, BF16)
    natural = pltpu.VMEM((rows, target_rank), BF16)
    xt = pltpu.VMEM((source_rank, points * source_rank), BF16)
    wide = pltpu.VMEM((target_rank, points * source_rank), BF16)
    narrow = pltpu.VMEM((target_rank, flat), BF16)
    acc = pltpu.VMEM((target_rank, source_rank), F32)
    env_buf = pltpu.VMEM((target_rank, source_rank), BF16)
    sems = pltpu.SemaphoreType.DMA((TILES,))
    side = pltpu.SemaphoreType.DMA((3,))
    params = pltpu.CompilerParams(vmem_limit_bytes=VMEM_LIMIT)
    first = pl.pallas_call(
        functools.partial(first_kernel, points),
        out_shape=(s_shape, s_shape, HBM(cb_shape.shape, BF16), y2_shape),
        in_specs=[place(SMEM)] + [place(HBM)] * 4,
        out_specs=(place(VMEM), place(VMEM), place(HBM), place(VMEM)),
        scratch_shapes=[x_buf, y_buf, cb, w, natural, acc, env_buf, sems, sems, side],
        compiler_params=params,
        name="first_step",
    )
    following = pl.pallas_call(
        next_kernel,
        out_shape=(s_shape, s_shape, HBM(cb_shape.shape, BF16)),
        in_specs=[place(SMEM), place(VMEM), place(HBM), place(HBM), place(VMEM)],
        out_specs=(place(VMEM), place(VMEM), place(HBM)),
        scratch_shapes=[x_buf, cb, w, natural, xt, wide, acc, env_buf, sems, sems, side],
        compiler_params=params,
        name="next_step",
    )
    last = pl.pallas_call(
        functools.partial(last_kernel, points),
        out_shape=jax.ShapeDtypeStruct((target_rank * points, target_rank), BF16),
        in_specs=[place(SMEM)] + [place(VMEM)] * 3 + [place(HBM)] * 3,
        out_specs=place(HBM),
        scratch_shapes=[cb, y_buf, narrow, env_buf, sems, pltpu.SemaphoreType.DMA((points // 2,))],
        compiler_params=params,
        name="projection",
    )
    return first, following, last


def exchange(kept, given, route):
    chunks, rows, width = kept.shape
    devices = lax.axis_size("mode")
    same_core = [list(range(c, devices, 2)) for c in range(2)]
    same_chip = [[d, d + 1] for d in range(0, devices, 2)]
    taken = lax.ppermute(given, "mode", [(d, d ^ 1) for d in range(devices)])
    chip = (kept.astype(F32) + taken.astype(F32)).astype(BF16)
    mine = lax.all_to_all(chip, "mode", 0, 0, axis_index_groups=same_core, tiled=True)
    summed = jnp.sum(mine.astype(F32), axis=0).astype(BF16)
    summed = lax.ppermute(summed, "cores", route)
    copies = jnp.broadcast_to(summed[None], (chunks, rows, width))
    whole = lax.all_to_all(copies, "mode", 0, 0, axis_index_groups=same_core, tiled=True)
    whole = lax.all_gather(whole, "mode", axis_index_groups=same_chip)
    return whole.reshape(2 * chunks, rows, width)


def body(x_cores, y_cores, left_boundary, right_boundary):
    _, source_rank, points, _ = x_cores.shape
    target_rank = left_boundary.shape[0]
    group = lax.axis_index("cores")
    core = lax.axis_index("mode") % 2
    x = in_hbm(x_cores.reshape(source_rank * points, source_rank))
    y = in_hbm(y_cores.reshape(target_rank * points, target_rank))
    left_boundary, right_boundary = in_hbm(left_boundary), in_hbm(right_boundary)
    first, following, last = step_calls(points, target_rank, source_rank)

    def role_at(position):
        role = jnp.where(group == position, LEFT, jnp.where(group == 3 - position, RIGHT, IDLE))
        if position == 1:
            role = jnp.where(group == 0, APPLY, role)
        return jnp.stack([role, core]).astype(jnp.int32)

    kept, given, cb, y2 = first(role_at(0), left_boundary, right_boundary, x, y)
    carried = [cb]
    envs = [exchange(kept, given, [(0, 1), (3, 2)])]
    for position, route in ((1, [(1, 2), (2, 1)]), (2, [(2, 3), (1, 0)])):
        kept, given, cb = following(role_at(position), envs[-1], left_boundary, x, y2)
        carried.append(cb)
        envs.append(exchange(kept, given, route))
    out = last(group.astype(jnp.int32).reshape(1), *envs, *map(in_hbm, carried))
    return out.reshape(1, target_rank, points, target_rank)


def solution(mesh):
    in_specs = (P("cores", None, "mode", None), P("cores", None, "mode", None), P(), P())
    out_specs = P("cores", None, "mode", None)
    return jax.shard_map(body, mesh=mesh, in_specs=in_specs, out_specs=out_specs, check_vma=False)
```

```python
import functools
import math

import jax
import jax.numpy as jnp
from jax import lax
from jax.experimental import pallas as pl
from jax.experimental.pallas import tpu as pltpu
from jax.sharding import PartitionSpec as P

EPSILON = 1e-06
TILES = 8
PARTS = 4
LANES = 128
VMEM_LIMIT = 36 * 1024 * 1024
BF16 = jnp.bfloat16
F32 = jnp.float32
NT = (((1,), (1,)), ((), ()))
TN = (((0,), (0,)), ((), ()))
SMEM, VMEM, HBM = pltpu.SMEM, pltpu.VMEM, pltpu.HBM
IDLE, LEFT, RIGHT, APPLY = 0, 1, 2, 3


def unpack(e_ref, env_ref):
    chunks, rows, width = e_ref.shape
    lanes = env_ref.shape[1] // width
    for j in range(chunks):
        r, k = j // lanes, j % lanes
        env_ref[rows * r : rows * (r + 1), width * k : width * (k + 1)] = e_ref[j]


def hand_out(acc, scale, core, kept, given):
    chunks, rows, width = kept.shape
    lanes = acc.shape[1] // width
    half = acc.shape[0] // 2
    for ref, owner in ((given, 1 - core), (kept, core)):
        start = pl.multiple_of(owner * half, half)
        for j in range(chunks):
            r, k = j // lanes, j % lanes
            value = acc[pl.ds(start + rows * r, rows), width * k : width * (k + 1)]
            if scale is not None:
                value = value * scale
            ref[j] = value.astype(BF16)


def scale_of(env):
    wide = env.astype(F32)
    return lax.rsqrt(jnp.mean(wide * wide) + EPSILON)


def tile_copies(x_ref, x_buf, sems):
    return [tile_copy(x_ref, x_buf, sems, t) for t in range(TILES)]


def tile_copy(x_ref, x_buf, sems, t):
    rows = x_buf.shape[0] // TILES
    part = block_of(t, rows)
    return pltpu.make_async_copy(x_ref.at[part], x_buf.at[part], sems.at[t])


def block_of(t, size):
    return pl.ds(t * size if isinstance(t, int) else pl.multiple_of(t * size, size), size)


def begin(copies):
    for copy in copies:
        copy.start()


def mode_major(y_buf, y2, points):
    step = y2.shape[0] // TILES

    @pl.loop(0, TILES)
    def _(t):
        y2[block_of(t, step), :] = y_buf[block_of(t, step * points), :].reshape(step, y2.shape[1])


def left_sum(env, x_ref, x, sems, y2, w, acc):
    width = env.shape[0]
    turned = env.T

    @pl.loop(0, y2.shape[1] // (2 * width))
    def _(i):
        lanes = block_of(i, 2 * width)
        w[:, lanes] = jnp.dot(turned, y2[:, lanes], preferred_element_type=F32).astype(BF16)

    rows = x.shape[0] // PARTS
    ranks = w.shape[0] // PARTS

    def term(t):
        for tile in range(TILES // PARTS):
            tile_copy(x_ref, x, sems, t * (TILES // PARTS) + tile).wait()
        own = w[block_of(t, ranks), :].reshape(rows, width)
        return lax.dot_general(own, x[block_of(t, rows), :], TN, preferred_element_type=F32)

    acc[...] = jnp.zeros_like(acc)

    @pl.loop(0, PARTS)
    def _(t):
        acc[...] += term(t)


def carry_back(env, x_ref, x, sems, natural, cb, cb_out, store_sems):
    rows = x.shape[0] // TILES
    ranks = cb.shape[0] // TILES
    turned = env.T

    @pl.loop(0, TILES)
    def _(t):
        tile_copy(x_ref, x, sems, t).wait()
        value = jnp.dot(x[block_of(t, rows), :], turned, preferred_element_type=F32)
        natural[...] = value.astype(BF16)
        cb[block_of(t, ranks), :] = natural[...].reshape(ranks, cb.shape[1])
        tile_copy(cb, cb_out, store_sems, t).start()


def right_sum(y2, cb, acc):
    half = cb.shape[0] // 2

    @pl.loop(0, 2)
    def _(n):
        acc[:, block_of(n, half)] = lax.dot_general(
            y2[...], cb[block_of(n, half), :], NT, preferred_element_type=F32
        )


def apply(env, x_ref, x, sems, xt, narrow, applied):
    source_rank = env.shape[1]
    rows = x.shape[0] // TILES
    ranks = xt.shape[0] // TILES

    @pl.loop(0, TILES)
    def _(t):
        tile_copy(x_ref, x, sems, t).wait()
        xt[block_of(t, ranks), :] = x[block_of(t, rows), :].reshape(ranks, xt.shape[1])

    @pl.loop(0, xt.shape[1] // source_rank)
    def _(i):
        lanes = block_of(i, source_rank)
        narrow[:, lanes] = jnp.dot(env, xt[:, lanes], preferred_element_type=F32).astype(BF16)

    blocks = applied.shape[1] // source_rank
    own = env.shape[0] // blocks

    @pl.loop(0, blocks)
    def _(j):
        applied[:, block_of(j, source_rank)] = narrow[block_of(j, own), :].reshape(source_rank, source_rank)


def first_kernel(
    points, role, lb, rb, x, y, kept, given, cb_out, y2, x_buf, y_buf, cb, w, natural, acc, env_buf, sems, store_sems, side
):
    load_y = pltpu.make_async_copy(y, y_buf, side.at[0])
    stores = tile_copies(cb, cb_out, store_sems)
    copies = tile_copies(x, x_buf, sems)

    @pl.when(role[0] == IDLE)
    def _():
        load_y.start()
        load_y.wait()
        mode_major(y_buf, y2, points)
        kept[...] = jnp.zeros_like(kept)
        given[...] = jnp.zeros_like(given)

    @pl.when(role[0] == LEFT)
    def _():
        load_y.start()
        load_env = pltpu.make_async_copy(lb, env_buf, side.at[2])
        load_env.start()
        load_y.wait()
        begin(copies)
        mode_major(y_buf, y2, points)
        load_env.wait()
        left_sum(env_buf[...], x, x_buf, sems, y2, w, acc)
        hand_out(acc, None, role[1], kept, given)

    @pl.when(role[0] == RIGHT)
    def _():
        load_env = pltpu.make_async_copy(rb, env_buf, side.at[2])
        load_env.start()
        load_y.start()
        begin(copies)
        load_env.wait()
        carry_back(env_buf[...], x, x_buf, sems, natural, cb, cb_out, store_sems)
        load_y.wait()
        mode_major(y_buf, y2, points)
        right_sum(y2, cb, acc)
        hand_out(acc, None, role[1], kept, given)
        for store in stores:
            store.wait()


def next_kernel(
    role, e, lb, x, y2, kept, given, cb_out, x_buf, cb, w, natural, xt, narrow, acc, env_buf, sems, store_sems, side
):
    stores = tile_copies(cb, cb_out, store_sems)
    copies = tile_copies(x, x_buf, sems)

    @pl.when(role[0] == IDLE)
    def _():
        kept[...] = jnp.zeros_like(kept)
        given[...] = jnp.zeros_like(given)

    @pl.when(role[0] == APPLY)
    def _():
        kept[...] = jnp.zeros_like(kept)
        given[...] = jnp.zeros_like(given)
        load_env = pltpu.make_async_copy(lb, env_buf, side.at[0])
        load_env.start()
        begin(copies)
        load_env.wait()
        apply(env_buf[...], x, x_buf, sems, xt, narrow, cb)
        for store in stores:
            store.start()
        for store in stores:
            store.wait()

    @pl.when(role[0] == LEFT)
    def _():
        begin(copies)
        unpack(e, env_buf)
        env = env_buf[...]
        left_sum(env, x, x_buf, sems, y2, w, acc)
        hand_out(acc, scale_of(env), role[1], kept, given)

    @pl.when(role[0] == RIGHT)
    def _():
        begin(copies)
        unpack(e, env_buf)
        env = env_buf[...]
        carry_back(env, x, x_buf, sems, natural, cb, cb_out, store_sems)
        right_sum(y2, cb, acc)
        hand_out(acc, scale_of(env), role[1], kept, given)
        for store in stores:
            store.wait()


def last_kernel(role, e1, e2, e3, cb0, cb1, cb2, out, cb, out_buf, narrow, env_buf, factor, sems, side):
    target_rank, source_rank = env_buf.shape
    block = out_buf.shape[0] // TILES
    lanes = cb.shape[1] // TILES

    def load(source, j):
        part = block_of(j, lanes)
        return pltpu.make_async_copy(source.at[:, part], cb.at[:, part], side.at[j])

    def store(t):
        part = block_of(t, block)
        return pltpu.make_async_copy(out_buf.at[part], out.at[part], sems.at[t])

    for group, source in ((0, cb1), (1, cb2), (2, cb1), (3, cb0)):

        @pl.when(role[0] == group)
        def _():
            for j in range(TILES):
                load(source, j).start()

    for group, e in ((1, e1), (2, e2)):

        @pl.when(role[0] == group)
        def _():
            unpack(e, env_buf)

    @pl.when((role[0] == 0) | (role[0] == 3))
    def _():
        unpack(e3, env_buf)

    other = jnp.where(role[0] == 1, scale_of(e2[...]), scale_of(e1[...]))
    inner = (role[0] == 1) | (role[0] == 2)
    env = env_buf[...]
    factor[0] = scale_of(env) * jnp.where(inner, other, 1.0) * (1.0 / math.sqrt(source_rank))

    @pl.when(role[0] == 0)
    def _():
        @pl.loop(0, TILES)
        def _(t):
            load(cb1, t).wait()
            value = lax.dot_general(cb[:, block_of(t, lanes)], env_buf[...], NT, preferred_element_type=F32)
            out_buf[block_of(t, block), :] = (value * factor[0]).astype(BF16)
            store(t).start()

    @pl.when(role[0] != 0)
    def _():
        @pl.loop(0, TILES)
        def _(j):
            load(cb1, j).wait()
            part = block_of(j, lanes)
            value = jnp.dot(env_buf[...], cb[:, part], preferred_element_type=F32)
            narrow[:, part] = (value * factor[0]).astype(BF16)

        @pl.loop(0, TILES)
        def _(t):
            own = narrow[block_of(t, target_rank // TILES), :]
            out_buf[block_of(t, block), :] = own.reshape(block, target_rank)
            store(t).start()

    for t in range(TILES):
        store(t).wait()


def place(kind):
    return pl.BlockSpec(memory_space=kind)


def in_hbm(array):
    return pltpu.with_memory_space_constraint(array, HBM)


def step_calls(points, target_rank, source_rank):
    chunk = (32, target_rank * source_rank // (64 * LANES), LANES)
    rows = source_rank * points
    flat = points * target_rank
    s_shape = jax.ShapeDtypeStruct(chunk, BF16)
    cb_shape = jax.ShapeDtypeStruct((source_rank, flat), BF16)
    y2_shape = jax.ShapeDtypeStruct((target_rank, flat), BF16)
    x_buf = pltpu.VMEM((rows, source_rank), BF16)
    cb = pltpu.VMEM(cb_shape.shape, BF16)
    y_buf = pltpu.VMEM((target_rank * points, target_rank), BF16)
    w = pltpu.VMEM(cb_shape.shape, BF16)
    natural = pltpu.VMEM((rows // TILES, target_rank), BF16)
    xt = pltpu.VMEM((source_rank, points * source_rank), BF16)
    wide = pltpu.VMEM((target_rank, points * source_rank), BF16)
    narrow = pltpu.VMEM((target_rank, flat), BF16)
    acc = pltpu.VMEM((target_rank, source_rank), F32)
    env_buf = pltpu.VMEM((target_rank, source_rank), BF16)
    sems = pltpu.SemaphoreType.DMA((TILES,))
    side = pltpu.SemaphoreType.DMA((3,))
    params = pltpu.CompilerParams(vmem_limit_bytes=VMEM_LIMIT)
    first = pl.pallas_call(
        functools.partial(first_kernel, points),
        out_shape=(s_shape, s_shape, HBM(cb_shape.shape, BF16), y2_shape),
        in_specs=[place(SMEM)] + [place(HBM)] * 4,
        out_specs=(place(VMEM), place(VMEM), place(HBM), place(VMEM)),
        scratch_shapes=[x_buf, y_buf, cb, w, natural, acc, env_buf, sems, sems, side],
        compiler_params=params,
        name="first_step",
    )
    following = pl.pallas_call(
        next_kernel,
        out_shape=(s_shape, s_shape, HBM(cb_shape.shape, BF16)),
        in_specs=[place(SMEM), place(VMEM), place(HBM), place(HBM), place(VMEM)],
        out_specs=(place(VMEM), place(VMEM), place(HBM)),
        scratch_shapes=[x_buf, cb, w, natural, xt, wide, acc, env_buf, sems, sems, side],
        compiler_params=params,
        name="next_step",
    )
    last = pl.pallas_call(
        last_kernel,
        out_shape=jax.ShapeDtypeStruct((target_rank * points, target_rank), BF16),
        in_specs=[place(SMEM)] + [place(VMEM)] * 3 + [place(HBM)] * 3,
        out_specs=place(HBM),
        scratch_shapes=[cb, y_buf, narrow, env_buf, pltpu.SMEM((1,), F32), sems, sems],
        compiler_params=params,
        name="projection",
    )
    return first, following, last


def exchange(kept, given, route):
    chunks, rows, width = kept.shape
    devices = lax.axis_size("mode")
    same_core = [list(range(c, devices, 2)) for c in range(2)]
    same_chip = [[d, d + 1] for d in range(0, devices, 2)]
    taken = lax.ppermute(given, "mode", [(d, d ^ 1) for d in range(devices)])
    chip = (kept.astype(F32) + taken.astype(F32)).astype(BF16)
    mine = lax.all_to_all(chip, "mode", 0, 0, axis_index_groups=same_core, tiled=True)
    summed = jnp.sum(mine.astype(F32), axis=0).astype(BF16)
    summed = lax.ppermute(summed, "cores", route)
    copies = jnp.broadcast_to(summed[None], (chunks, rows, width))
    whole = lax.all_to_all(copies, "mode", 0, 0, axis_index_groups=same_core, tiled=True)
    whole = lax.all_gather(whole, "mode", axis_index_groups=same_chip)
    return whole.reshape(2 * chunks, rows, width)


def body(x_cores, y_cores, left_boundary, right_boundary):
    _, source_rank, points, _ = x_cores.shape
    target_rank = left_boundary.shape[0]
    group = lax.axis_index("cores")
    core = lax.axis_index("mode") % 2
    x = in_hbm(x_cores.reshape(source_rank * points, source_rank))
    y = in_hbm(y_cores.reshape(target_rank * points, target_rank))
    left_boundary, right_boundary = in_hbm(left_boundary), in_hbm(right_boundary)
    first, following, last = step_calls(points, target_rank, source_rank)

    def role_at(position):
        role = jnp.where(group == position, LEFT, jnp.where(group == 3 - position, RIGHT, IDLE))
        if position == 1:
            role = jnp.where(group == 0, APPLY, role)
        return jnp.stack([role, core]).astype(jnp.int32)

    kept, given, cb, y2 = first(role_at(0), left_boundary, right_boundary, x, y)
    carried = [cb]
    envs = [exchange(kept, given, [(0, 1), (3, 2)])]
    for position, route in ((1, [(1, 2), (2, 1)]), (2, [(2, 3), (1, 0)])):
        kept, given, cb = following(role_at(position), envs[-1], left_boundary, x, y2)
        carried.append(cb)
        envs.append(exchange(kept, given, route))
    out = last(group.astype(jnp.int32).reshape(1), *envs, *map(in_hbm, carried))
    return out.reshape(1, target_rank, points, target_rank)


def solution(mesh):
    in_specs = (P("cores", None, "mode", None), P("cores", None, "mode", None), P(), P())
    out_specs = P("cores", None, "mode", None)
    return jax.shard_map(body, mesh=mesh, in_specs=in_specs, out_specs=out_specs, check_vma=False)
```

```python
import functools
import math

import jax
import jax.numpy as jnp
from jax import lax
from jax.experimental import pallas as pl
from jax.experimental.pallas import tpu as pltpu
from jax.sharding import PartitionSpec as P

EPSILON = 1e-06
TILES = 8
PARTS = 2
WINDOW = 3
LANES = 128
VMEM_LIMIT = 36 * 1024 * 1024
BF16 = jnp.bfloat16
F32 = jnp.float32
NT = (((1,), (1,)), ((), ()))
TN = (((0,), (0,)), ((), ()))
SMEM, VMEM, HBM = pltpu.SMEM, pltpu.VMEM, pltpu.HBM
IDLE, LEFT, RIGHT, APPLY = 0, 1, 2, 3


def unpack(own, others, core, env_ref):
    chunks, rows, width = own.shape
    lanes = env_ref.shape[1] // width
    half = env_ref.shape[0] // 2
    for ref, owner in ((own, core), (others, 1 - core)):
        for j in range(chunks):
            r, k = j // lanes, j % lanes
            start = pl.multiple_of(owner * half + rows * r, rows)
            env_ref[pl.ds(start, rows), width * k : width * (k + 1)] = ref[j]


def hand_out(acc, scale, core, kept, given):
    chunks, rows, width = kept.shape
    lanes = acc.shape[1] // width
    half = acc.shape[0] // 2
    for ref, owner in ((given, 1 - core), (kept, core)):
        start = pl.multiple_of(owner * half, half)
        for j in range(chunks):
            r, k = j // lanes, j % lanes
            value = acc[pl.ds(start + rows * r, rows), width * k : width * (k + 1)]
            if scale is not None:
                value = value * scale
            ref[j] = value.astype(BF16)


def scale_of(*parts):
    wide = [part.astype(F32) for part in parts]
    return lax.rsqrt(sum(jnp.mean(value * value) for value in wide) / len(parts) + EPSILON)


def tile_copies(x_ref, x_buf, sems):
    return [tile_copy(x_ref, x_buf, sems, t) for t in range(TILES)]


def tile_copy(x_ref, x_buf, sems, t):
    rows = x_buf.shape[0] // TILES
    part = block_of(t, rows)
    return pltpu.make_async_copy(x_ref.at[part], x_buf.at[part], sems.at[t])


def block_of(t, size):
    return pl.ds(t * size if isinstance(t, int) else pl.multiple_of(t * size, size), size)


def begin(copies):
    for copy in copies:
        copy.start()


def mode_major(y_buf, y2, points):
    step = y2.shape[0] // TILES

    @pl.loop(0, TILES)
    def _(t):
        y2[block_of(t, step), :] = y_buf[block_of(t, step * points), :].reshape(step, y2.shape[1])


def left_sum(env, x_ref, x, sems, y2, w, acc):
    width = env.shape[0]
    turned = env.T

    @pl.loop(0, y2.shape[1] // (2 * width))
    def _(i):
        lanes = block_of(i, 2 * width)
        w[:, lanes] = jnp.dot(turned, y2[:, lanes], preferred_element_type=F32).astype(BF16)

    rows = x.shape[0] // PARTS
    ranks = w.shape[0] // PARTS

    def term(t):
        for tile in range(TILES // PARTS):
            tile_copy(x_ref, x, sems, t * (TILES // PARTS) + tile).wait()
        own = w[block_of(t, ranks), :].reshape(rows, width)
        return lax.dot_general(own, x[block_of(t, rows), :], TN, preferred_element_type=F32)

    acc[...] = jnp.zeros_like(acc)

    @pl.loop(0, PARTS)
    def _(t):
        acc[...] += term(t)


def carry_back(env, window, x_ref, x, sems, natural, cb, cb_out, store_sems):
    rows = x.shape[0] // TILES
    ranks = cb.shape[0] // TILES
    turned = env.T

    @pl.loop(0, TILES)
    def _(t):
        tile_copy(x_ref, x, sems, t).wait()

        if window < TILES:

            @pl.when(t + window < TILES)
            def _():
                tile_copy(x_ref, x, sems, t + window).start()

        value = jnp.dot(x[block_of(t, rows), :], turned, preferred_element_type=F32)
        natural[...] = value.astype(BF16)
        cb[block_of(t, ranks), :] = natural[...].reshape(ranks, cb.shape[1])
        tile_copy(cb, cb_out, store_sems, t).start()


def right_sum(y2, cb, acc):
    half = cb.shape[0] // 2

    @pl.loop(0, 2)
    def _(n):
        acc[:, block_of(n, half)] = lax.dot_general(
            y2[...], cb[block_of(n, half), :], NT, preferred_element_type=F32
        )


def apply(env, x_ref, x, sems, xt, narrow, applied):
    source_rank = env.shape[1]
    rows = x.shape[0] // TILES
    ranks = xt.shape[0] // TILES

    @pl.loop(0, TILES)
    def _(t):
        tile_copy(x_ref, x, sems, t).wait()
        xt[block_of(t, ranks), :] = x[block_of(t, rows), :].reshape(ranks, xt.shape[1])

    @pl.loop(0, xt.shape[1] // source_rank)
    def _(i):
        lanes = block_of(i, source_rank)
        narrow[:, lanes] = jnp.dot(env, xt[:, lanes], preferred_element_type=F32).astype(BF16)

    blocks = applied.shape[1] // source_rank
    own = env.shape[0] // blocks

    @pl.loop(0, blocks)
    def _(j):
        applied[:, block_of(j, source_rank)] = narrow[block_of(j, own), :].reshape(source_rank, source_rank)


def first_kernel(
    points, role, lb, rb, x, y, kept, given, cb_out, y2, x_buf, y_buf, cb, w, natural, acc, env_buf, sems, store_sems, side
):
    load_y = pltpu.make_async_copy(y, y_buf, side.at[0])
    stores = tile_copies(cb, cb_out, store_sems)
    copies = tile_copies(x, x_buf, sems)

    @pl.when(role[0] == IDLE)
    def _():
        load_y.start()
        load_y.wait()
        mode_major(y_buf, y2, points)
        kept[...] = jnp.zeros_like(kept)
        given[...] = jnp.zeros_like(given)

    @pl.when(role[0] == LEFT)
    def _():
        load_y.start()
        load_env = pltpu.make_async_copy(lb, env_buf, side.at[2])
        load_env.start()
        load_y.wait()
        begin(copies)
        mode_major(y_buf, y2, points)
        load_env.wait()
        left_sum(env_buf[...], x, x_buf, sems, y2, w, acc)
        hand_out(acc, None, role[1], kept, given)

    @pl.when(role[0] == RIGHT)
    def _():
        load_env = pltpu.make_async_copy(rb, env_buf, side.at[2])
        load_env.start()
        load_y.start()
        begin(copies[:WINDOW])
        load_env.wait()
        carry_back(env_buf[...], WINDOW, x, x_buf, sems, natural, cb, cb_out, store_sems)
        load_y.wait()
        mode_major(y_buf, y2, points)
        right_sum(y2, cb, acc)
        hand_out(acc, None, role[1], kept, given)
        for store in stores:
            store.wait()


def next_kernel(
    role, e, f, lb, x, y2, kept, given, cb_out, x_buf, cb, w, natural, xt, narrow, acc, env_buf, sems, store_sems, side
):
    stores = tile_copies(cb, cb_out, store_sems)
    copies = tile_copies(x, x_buf, sems)

    @pl.when(role[0] == IDLE)
    def _():
        kept[...] = jnp.zeros_like(kept)
        given[...] = jnp.zeros_like(given)

    @pl.when(role[0] == APPLY)
    def _():
        kept[...] = jnp.zeros_like(kept)
        given[...] = jnp.zeros_like(given)
        load_env = pltpu.make_async_copy(lb, env_buf, side.at[0])
        load_env.start()
        begin(copies)
        load_env.wait()
        apply(env_buf[...], x, x_buf, sems, xt, narrow, cb)
        for store in stores:
            store.start()
        for store in stores:
            store.wait()

    @pl.when(role[0] == LEFT)
    def _():
        begin(copies)
        unpack(e, f, role[1], env_buf)
        env = env_buf[...]
        left_sum(env, x, x_buf, sems, y2, w, acc)
        hand_out(acc, scale_of(env), role[1], kept, given)

    @pl.when(role[0] == RIGHT)
    def _():
        begin(copies)
        unpack(e, f, role[1], env_buf)
        env = env_buf[...]
        carry_back(env, TILES, x, x_buf, sems, natural, cb, cb_out, store_sems)
        right_sum(y2, cb, acc)
        hand_out(acc, scale_of(env), role[1], kept, given)
        for store in stores:
            store.wait()


def last_kernel(
    role, e1, f1, e2, f2, e3, f3, cb0, cb1, cb2, out, cb, out_buf, narrow, env_buf, factor, sems, side
):
    target_rank, source_rank = env_buf.shape
    block = out_buf.shape[0] // TILES
    lanes = cb.shape[1] // TILES

    def load(source, j):
        part = block_of(j, lanes)
        return pltpu.make_async_copy(source.at[:, part], cb.at[:, part], side.at[j])

    def store(t):
        part = block_of(t, block)
        return pltpu.make_async_copy(out_buf.at[part], out.at[part], sems.at[t])

    for group, source in ((0, cb1), (1, cb2), (2, cb1), (3, cb0)):

        @pl.when(role[0] == group)
        def _():
            for j in range(TILES):
                load(source, j).start()

    for group, e, f in ((1, e1, f1), (2, e2, f2)):

        @pl.when(role[0] == group)
        def _():
            unpack(e, f, role[1], env_buf)

    @pl.when((role[0] == 0) | (role[0] == 3))
    def _():
        unpack(e3, f3, role[1], env_buf)

    other = jnp.where(role[0] == 1, scale_of(e2[...], f2[...]), scale_of(e1[...], f1[...]))
    inner = (role[0] == 1) | (role[0] == 2)
    env = env_buf[...]
    factor[0] = scale_of(env) * jnp.where(inner, other, 1.0) * (1.0 / math.sqrt(source_rank))

    @pl.when(role[0] == 0)
    def _():
        @pl.loop(0, TILES)
        def _(t):
            load(cb1, t).wait()
            value = lax.dot_general(cb[:, block_of(t, lanes)], env_buf[...], NT, preferred_element_type=F32)
            out_buf[block_of(t, block), :] = (value * factor[0]).astype(BF16)
            store(t).start()

    @pl.when(role[0] != 0)
    def _():
        @pl.loop(0, TILES)
        def _(j):
            load(cb1, j).wait()
            part = block_of(j, lanes)
            value = jnp.dot(env_buf[...], cb[:, part], preferred_element_type=F32)
            narrow[:, part] = (value * factor[0]).astype(BF16)

        @pl.loop(0, TILES)
        def _(t):
            own = narrow[block_of(t, target_rank // TILES), :]
            out_buf[block_of(t, block), :] = own.reshape(block, target_rank)
            store(t).start()

    for t in range(TILES):
        store(t).wait()


def place(kind):
    return pl.BlockSpec(memory_space=kind)


def in_hbm(array):
    return pltpu.with_memory_space_constraint(array, HBM)


def step_calls(points, target_rank, source_rank):
    chunk = (32, target_rank * source_rank // (64 * LANES), LANES)
    rows = source_rank * points
    flat = points * target_rank
    s_shape = jax.ShapeDtypeStruct(chunk, BF16)
    cb_shape = jax.ShapeDtypeStruct((source_rank, flat), BF16)
    y2_shape = jax.ShapeDtypeStruct((target_rank, flat), BF16)
    x_buf = pltpu.VMEM((rows, source_rank), BF16)
    cb = pltpu.VMEM(cb_shape.shape, BF16)
    y_buf = pltpu.VMEM((target_rank * points, target_rank), BF16)
    w = pltpu.VMEM(cb_shape.shape, BF16)
    natural = pltpu.VMEM((rows // TILES, target_rank), BF16)
    xt = pltpu.VMEM((source_rank, points * source_rank), BF16)
    wide = pltpu.VMEM((target_rank, points * source_rank), BF16)
    narrow = pltpu.VMEM((target_rank, flat), BF16)
    acc = pltpu.VMEM((target_rank, source_rank), F32)
    env_buf = pltpu.VMEM((target_rank, source_rank), BF16)
    sems = pltpu.SemaphoreType.DMA((TILES,))
    side = pltpu.SemaphoreType.DMA((3,))
    params = pltpu.CompilerParams(vmem_limit_bytes=VMEM_LIMIT)
    first = pl.pallas_call(
        functools.partial(first_kernel, points),
        out_shape=(s_shape, s_shape, HBM(cb_shape.shape, BF16), y2_shape),
        in_specs=[place(SMEM)] + [place(HBM)] * 4,
        out_specs=(place(VMEM), place(VMEM), place(HBM), place(VMEM)),
        scratch_shapes=[x_buf, y_buf, cb, w, natural, acc, env_buf, sems, sems, side],
        compiler_params=params,
        name="first_step",
    )
    following = pl.pallas_call(
        next_kernel,
        out_shape=(s_shape, s_shape, HBM(cb_shape.shape, BF16)),
        in_specs=[place(SMEM), place(VMEM), place(VMEM), place(HBM), place(HBM), place(VMEM)],
        out_specs=(place(VMEM), place(VMEM), place(HBM)),
        scratch_shapes=[x_buf, cb, w, natural, xt, wide, acc, env_buf, sems, sems, side],
        compiler_params=params,
        name="next_step",
    )
    last = pl.pallas_call(
        last_kernel,
        out_shape=jax.ShapeDtypeStruct((target_rank * points, target_rank), BF16),
        in_specs=[place(SMEM)] + [place(VMEM)] * 6 + [place(HBM)] * 3,
        out_specs=place(HBM),
        scratch_shapes=[cb, y_buf, narrow, env_buf, pltpu.SMEM((1,), F32), sems, sems],
        compiler_params=params,
        name="projection",
    )
    return first, following, last


def exchange(kept, given, route):
    chunks, rows, width = kept.shape
    devices = lax.axis_size("mode")
    same_core = [list(range(c, devices, 2)) for c in range(2)]
    neighbour = [(d, d ^ 1) for d in range(devices)]
    taken = lax.ppermute(given, "mode", neighbour)
    chip = (kept.astype(F32) + taken.astype(F32)).astype(BF16)
    mine = lax.all_to_all(chip, "mode", 0, 0, axis_index_groups=same_core, tiled=True)
    summed = jnp.sum(mine.astype(F32), axis=0).astype(BF16)
    summed = lax.ppermute(summed, "cores", route)
    copies = jnp.broadcast_to(summed[None], (chunks, rows, width))
    whole = lax.all_to_all(copies, "mode", 0, 0, axis_index_groups=same_core, tiled=True)
    return whole, lax.ppermute(whole, "mode", neighbour)


def body(x_cores, y_cores, left_boundary, right_boundary):
    _, source_rank, points, _ = x_cores.shape
    target_rank = left_boundary.shape[0]
    group = lax.axis_index("cores")
    core = lax.axis_index("mode") % 2
    x = in_hbm(x_cores.reshape(source_rank * points, source_rank))
    y = in_hbm(y_cores.reshape(target_rank * points, target_rank))
    left_boundary, right_boundary = in_hbm(left_boundary), in_hbm(right_boundary)
    first, following, last = step_calls(points, target_rank, source_rank)

    def role_at(position):
        role = jnp.where(group == position, LEFT, jnp.where(group == 3 - position, RIGHT, IDLE))
        if position == 1:
            role = jnp.where(group == 0, APPLY, role)
        return jnp.stack([role, core]).astype(jnp.int32)

    kept, given, cb, y2 = first(role_at(0), left_boundary, right_boundary, x, y)
    carried = [cb]
    envs = [exchange(kept, given, [(0, 1), (3, 2)])]
    for position, route in ((1, [(1, 2), (2, 1)]), (2, [(2, 3), (1, 0)])):
        kept, given, cb = following(role_at(position), *envs[-1], left_boundary, x, y2)
        carried.append(cb)
        envs.append(exchange(kept, given, route))
    out = last(jnp.stack([group, core]).astype(jnp.int32), *sum(envs, ()), *map(in_hbm, carried))
    return out.reshape(1, target_rank, points, target_rank)


def solution(mesh):
    in_specs = (P("cores", None, "mode", None), P("cores", None, "mode", None), P(), P())
    out_specs = P("cores", None, "mode", None)
    return jax.shard_map(body, mesh=mesh, in_specs=in_specs, out_specs=out_specs, check_vma=False)
```

```python
import functools
import math

import jax
import jax.numpy as jnp
from jax import lax
from jax.experimental import pallas as pl
from jax.experimental.pallas import tpu as pltpu
from jax.sharding import PartitionSpec as P

EPSILON = 1e-06
TILES = 8
PARTS = 2
WINDOW = 3
LANES = 128
VMEM_LIMIT = 36 * 1024 * 1024
BF16 = jnp.bfloat16
F32 = jnp.float32
NT = (((1,), (1,)), ((), ()))
TN = (((0,), (0,)), ((), ()))
SMEM, VMEM, HBM = pltpu.SMEM, pltpu.VMEM, pltpu.HBM
IDLE, LEFT, RIGHT, APPLY = 0, 1, 2, 3


def unpack(own, others, core, env_ref):
    chunks, rows, width = own.shape
    lanes = env_ref.shape[1] // width
    half = env_ref.shape[0] // 2
    for ref, owner in ((own, 1 - core), (others, core)):
        for j in range(chunks):
            r, k = j // lanes, j % lanes
            start = pl.multiple_of(owner * half + rows * r, rows)
            env_ref[pl.ds(start, rows), width * k : width * (k + 1)] = ref[j]


def hand_out(acc, scale, core, kept, given):
    chunks, rows, width = kept.shape
    lanes = acc.shape[1] // width
    half = acc.shape[0] // 2
    for ref, owner in ((given, 1 - core), (kept, core)):
        start = pl.multiple_of(owner * half, half)
        for j in range(chunks):
            r, k = j // lanes, j % lanes
            value = acc[pl.ds(start + rows * r, rows), width * k : width * (k + 1)]
            if scale is not None:
                value = value * scale
            ref[j] = value.astype(BF16)


def scale_of(*parts):
    wide = [part.astype(F32) for part in parts]
    return lax.rsqrt(sum(jnp.mean(value * value) for value in wide) / len(parts) + EPSILON)


def tile_copies(x_ref, x_buf, sems):
    return [tile_copy(x_ref, x_buf, sems, t) for t in range(TILES)]


def tile_copy(x_ref, x_buf, sems, t):
    rows = x_buf.shape[0] // TILES
    part = block_of(t, rows)
    return pltpu.make_async_copy(x_ref.at[part], x_buf.at[part], sems.at[t])


def block_of(t, size):
    return pl.ds(t * size if isinstance(t, int) else pl.multiple_of(t * size, size), size)


def begin(copies):
    for copy in copies:
        copy.start()


def mode_major(y_buf, y2, points):
    step = y2.shape[0] // TILES

    @pl.loop(0, TILES)
    def _(t):
        y2[block_of(t, step), :] = y_buf[block_of(t, step * points), :].reshape(step, y2.shape[1])


def left_sum(env, x_ref, x, sems, y2, w, acc):
    width = env.shape[0]
    turned = env.T

    @pl.loop(0, y2.shape[1] // (2 * width))
    def _(i):
        lanes = block_of(i, 2 * width)
        w[:, lanes] = jnp.dot(turned, y2[:, lanes], preferred_element_type=F32).astype(BF16)

    rows = x.shape[0] // PARTS
    ranks = w.shape[0] // PARTS

    def term(t):
        for tile in range(TILES // PARTS):
            tile_copy(x_ref, x, sems, t * (TILES // PARTS) + tile).wait()
        own = w[block_of(t, ranks), :].reshape(rows, width)
        return lax.dot_general(own, x[block_of(t, rows), :], TN, preferred_element_type=F32)

    acc[...] = jnp.zeros_like(acc)

    @pl.loop(0, PARTS)
    def _(t):
        acc[...] += term(t)


def carry_back(env, window, x_ref, x, sems, natural, cb, cb_out, store_sems):
    rows = x.shape[0] // TILES
    ranks = cb.shape[0] // TILES
    turned = env.T

    @pl.loop(0, TILES)
    def _(t):
        tile_copy(x_ref, x, sems, t).wait()

        if window < TILES:

            @pl.when(t + window < TILES)
            def _():
                tile_copy(x_ref, x, sems, t + window).start()

        value = jnp.dot(x[block_of(t, rows), :], turned, preferred_element_type=F32)
        natural[...] = value.astype(BF16)
        cb[block_of(t, ranks), :] = natural[...].reshape(ranks, cb.shape[1])
        tile_copy(cb, cb_out, store_sems, t).start()


def right_sum(y2, cb, acc):
    half = cb.shape[0] // 2

    @pl.loop(0, 2)
    def _(n):
        acc[:, block_of(n, half)] = lax.dot_general(
            y2[...], cb[block_of(n, half), :], NT, preferred_element_type=F32
        )


def apply(env, x_ref, x, sems, xt, narrow, applied):
    source_rank = env.shape[1]
    rows = x.shape[0] // TILES
    ranks = xt.shape[0] // TILES

    @pl.loop(0, TILES)
    def _(t):
        tile_copy(x_ref, x, sems, t).wait()
        xt[block_of(t, ranks), :] = x[block_of(t, rows), :].reshape(ranks, xt.shape[1])

    @pl.loop(0, xt.shape[1] // source_rank)
    def _(i):
        lanes = block_of(i, source_rank)
        narrow[:, lanes] = jnp.dot(env, xt[:, lanes], preferred_element_type=F32).astype(BF16)

    blocks = applied.shape[1] // source_rank
    own = env.shape[0] // blocks

    @pl.loop(0, blocks)
    def _(j):
        applied[:, block_of(j, source_rank)] = narrow[block_of(j, own), :].reshape(source_rank, source_rank)


def first_kernel(
    points, role, lb, rb, x, y, kept, given, cb_out, y2, x_buf, y_buf, cb, w, natural, acc, env_buf, sems, store_sems, side
):
    load_y = pltpu.make_async_copy(y, y_buf, side.at[0])
    stores = tile_copies(cb, cb_out, store_sems)
    copies = tile_copies(x, x_buf, sems)

    @pl.when(role[0] == IDLE)
    def _():
        load_y.start()
        load_y.wait()
        mode_major(y_buf, y2, points)
        kept[...] = jnp.zeros_like(kept)
        given[...] = jnp.zeros_like(given)

    @pl.when(role[0] == LEFT)
    def _():
        load_y.start()
        load_env = pltpu.make_async_copy(lb, env_buf, side.at[2])
        load_env.start()
        load_y.wait()
        begin(copies)
        mode_major(y_buf, y2, points)
        load_env.wait()
        left_sum(env_buf[...], x, x_buf, sems, y2, w, acc)
        hand_out(acc, None, role[1], kept, given)

    @pl.when(role[0] == RIGHT)
    def _():
        load_env = pltpu.make_async_copy(rb, env_buf, side.at[2])
        load_env.start()
        load_y.start()
        begin(copies[:WINDOW])
        load_env.wait()
        carry_back(env_buf[...], WINDOW, x, x_buf, sems, natural, cb, cb_out, store_sems)
        load_y.wait()
        mode_major(y_buf, y2, points)
        right_sum(y2, cb, acc)
        hand_out(acc, None, role[1], kept, given)
        for store in stores:
            store.wait()


def next_kernel(
    role, e, f, lb, x, y2, kept, given, cb_out, x_buf, cb, w, natural, xt, narrow, acc, env_buf, sems, store_sems, side
):
    stores = tile_copies(cb, cb_out, store_sems)
    copies = tile_copies(x, x_buf, sems)

    @pl.when(role[0] == IDLE)
    def _():
        kept[...] = jnp.zeros_like(kept)
        given[...] = jnp.zeros_like(given)

    @pl.when(role[0] == APPLY)
    def _():
        kept[...] = jnp.zeros_like(kept)
        given[...] = jnp.zeros_like(given)
        load_env = pltpu.make_async_copy(lb, env_buf, side.at[0])
        load_env.start()
        begin(copies)
        load_env.wait()
        apply(env_buf[...], x, x_buf, sems, xt, narrow, cb)
        for store in stores:
            store.start()
        for store in stores:
            store.wait()

    @pl.when(role[0] == LEFT)
    def _():
        begin(copies)
        unpack(e, f, role[1], env_buf)
        env = env_buf[...]
        left_sum(env, x, x_buf, sems, y2, w, acc)
        hand_out(acc, scale_of(env), role[1], kept, given)

    @pl.when(role[0] == RIGHT)
    def _():
        begin(copies)
        unpack(e, f, role[1], env_buf)
        env = env_buf[...]
        carry_back(env, TILES, x, x_buf, sems, natural, cb, cb_out, store_sems)
        right_sum(y2, cb, acc)
        hand_out(acc, scale_of(env), role[1], kept, given)
        for store in stores:
            store.wait()


def last_kernel(
    role, e1, f1, e2, f2, e3, f3, cb0, cb1, cb2, out, cb, out_buf, narrow, env_buf, factor, sems, side
):
    target_rank, source_rank = env_buf.shape
    block = out_buf.shape[0] // TILES
    lanes = cb.shape[1] // TILES

    def load(source, j):
        part = block_of(j, lanes)
        return pltpu.make_async_copy(source.at[:, part], cb.at[:, part], side.at[j])

    def store(t):
        part = block_of(t, block)
        return pltpu.make_async_copy(out_buf.at[part], out.at[part], sems.at[t])

    for group, source in ((0, cb1), (1, cb2), (2, cb1), (3, cb0)):

        @pl.when(role[0] == group)
        def _():
            for j in range(TILES):
                load(source, j).start()

    for group, e, f in ((1, e1, f1), (2, e2, f2)):

        @pl.when(role[0] == group)
        def _():
            unpack(e, f, role[1], env_buf)

    @pl.when((role[0] == 0) | (role[0] == 3))
    def _():
        unpack(e3, f3, role[1], env_buf)

    other = jnp.where(role[0] == 1, scale_of(e2[...], f2[...]), scale_of(e1[...], f1[...]))
    inner = (role[0] == 1) | (role[0] == 2)
    env = env_buf[...]
    factor[0] = scale_of(env) * jnp.where(inner, other, 1.0) * (1.0 / math.sqrt(source_rank))

    @pl.when(role[0] == 0)
    def _():
        @pl.loop(0, TILES)
        def _(t):
            load(cb1, t).wait()
            value = lax.dot_general(cb[:, block_of(t, lanes)], env_buf[...], NT, preferred_element_type=F32)
            out_buf[block_of(t, block), :] = (value * factor[0]).astype(BF16)
            store(t).start()

    @pl.when(role[0] != 0)
    def _():
        @pl.loop(0, TILES)
        def _(j):
            load(cb1, j).wait()
            part = block_of(j, lanes)
            value = jnp.dot(env_buf[...], cb[:, part], preferred_element_type=F32)
            narrow[:, part] = (value * factor[0]).astype(BF16)

        @pl.loop(0, TILES)
        def _(t):
            own = narrow[block_of(t, target_rank // TILES), :]
            out_buf[block_of(t, block), :] = own.reshape(block, target_rank)
            store(t).start()

    for t in range(TILES):
        store(t).wait()


def place(kind):
    return pl.BlockSpec(memory_space=kind)


def in_hbm(array):
    return pltpu.with_memory_space_constraint(array, HBM)


def step_calls(points, target_rank, source_rank):
    chunk = (32, target_rank * source_rank // (64 * LANES), LANES)
    rows = source_rank * points
    flat = points * target_rank
    s_shape = jax.ShapeDtypeStruct(chunk, BF16)
    cb_shape = jax.ShapeDtypeStruct((source_rank, flat), BF16)
    y2_shape = jax.ShapeDtypeStruct((target_rank, flat), BF16)
    x_buf = pltpu.VMEM((rows, source_rank), BF16)
    cb = pltpu.VMEM(cb_shape.shape, BF16)
    y_buf = pltpu.VMEM((target_rank * points, target_rank), BF16)
    w = pltpu.VMEM(cb_shape.shape, BF16)
    natural = pltpu.VMEM((rows // TILES, target_rank), BF16)
    xt = pltpu.VMEM((source_rank, points * source_rank), BF16)
    wide = pltpu.VMEM((target_rank, points * source_rank), BF16)
    narrow = pltpu.VMEM((target_rank, flat), BF16)
    acc = pltpu.VMEM((target_rank, source_rank), F32)
    env_buf = pltpu.VMEM((target_rank, source_rank), BF16)
    sems = pltpu.SemaphoreType.DMA((TILES,))
    side = pltpu.SemaphoreType.DMA((3,))
    params = pltpu.CompilerParams(vmem_limit_bytes=VMEM_LIMIT)
    first = pl.pallas_call(
        functools.partial(first_kernel, points),
        out_shape=(s_shape, s_shape, HBM(cb_shape.shape, BF16), y2_shape),
        in_specs=[place(SMEM)] + [place(HBM)] * 4,
        out_specs=(place(VMEM), place(VMEM), place(HBM), place(VMEM)),
        scratch_shapes=[x_buf, y_buf, cb, w, natural, acc, env_buf, sems, sems, side],
        compiler_params=params,
        name="first_step",
    )
    following = pl.pallas_call(
        next_kernel,
        out_shape=(s_shape, s_shape, HBM(cb_shape.shape, BF16)),
        in_specs=[place(SMEM), place(VMEM), place(VMEM), place(HBM), place(HBM), place(VMEM)],
        out_specs=(place(VMEM), place(VMEM), place(HBM)),
        scratch_shapes=[x_buf, cb, w, natural, xt, wide, acc, env_buf, sems, sems, side],
        compiler_params=params,
        name="next_step",
    )
    last = pl.pallas_call(
        last_kernel,
        out_shape=jax.ShapeDtypeStruct((target_rank * points, target_rank), BF16),
        in_specs=[place(SMEM)] + [place(VMEM)] * 6 + [place(HBM)] * 3,
        out_specs=place(HBM),
        scratch_shapes=[cb, y_buf, narrow, env_buf, pltpu.SMEM((1,), F32), sems, sems],
        compiler_params=params,
        name="projection",
    )
    return first, following, last


def exchange(kept, given, route):
    chunks, rows, width = kept.shape
    devices = lax.axis_size("mode")
    same_core = [list(range(c, devices, 2)) for c in range(2)]
    neighbour = [(d, d ^ 1) for d in range(devices)]
    taken = lax.ppermute(given, "mode", neighbour)
    chip = (kept.astype(F32) + taken.astype(F32)).astype(BF16)
    mine = lax.all_to_all(chip, "mode", 0, 0, axis_index_groups=same_core, tiled=True)
    summed = jnp.sum(mine.astype(F32), axis=0).astype(BF16)
    hops = [
        (source * devices + d, target * devices + (d ^ 1)) for source, target in route for d in range(devices)
    ]
    summed = lax.ppermute(summed, ("cores", "mode"), hops)
    copies = jnp.broadcast_to(summed[None], (chunks, rows, width))
    whole = lax.all_to_all(copies, "mode", 0, 0, axis_index_groups=same_core, tiled=True)
    return whole, lax.ppermute(whole, "mode", neighbour)


def body(x_cores, y_cores, left_boundary, right_boundary):
    _, source_rank, points, _ = x_cores.shape
    target_rank = left_boundary.shape[0]
    group = lax.axis_index("cores")
    core = lax.axis_index("mode") % 2
    x = in_hbm(x_cores.reshape(source_rank * points, source_rank))
    y = in_hbm(y_cores.reshape(target_rank * points, target_rank))
    left_boundary, right_boundary = in_hbm(left_boundary), in_hbm(right_boundary)
    first, following, last = step_calls(points, target_rank, source_rank)

    def role_at(position):
        role = jnp.where(group == position, LEFT, jnp.where(group == 3 - position, RIGHT, IDLE))
        if position == 1:
            role = jnp.where(group == 0, APPLY, role)
        return jnp.stack([role, core]).astype(jnp.int32)

    kept, given, cb, y2 = first(role_at(0), left_boundary, right_boundary, x, y)
    carried = [cb]
    envs = [exchange(kept, given, [(0, 1), (3, 2)])]
    for position, route in ((1, [(1, 2), (2, 1)]), (2, [(2, 3), (1, 0)])):
        kept, given, cb = following(role_at(position), *envs[-1], left_boundary, x, y2)
        carried.append(cb)
        envs.append(exchange(kept, given, route))
    out = last(jnp.stack([group, core]).astype(jnp.int32), *sum(envs, ()), *map(in_hbm, carried))
    return out.reshape(1, target_rank, points, target_rank)


def solution(mesh):
    in_specs = (P("cores", None, "mode", None), P("cores", None, "mode", None), P(), P())
    out_specs = P("cores", None, "mode", None)
    return jax.shard_map(body, mesh=mesh, in_specs=in_specs, out_specs=out_specs, check_vma=False)
```

```python
import functools
import math

import jax
import jax.numpy as jnp
from jax import lax
from jax.experimental import pallas as pl
from jax.experimental.pallas import tpu as pltpu
from jax.sharding import PartitionSpec as P

EPSILON = 1e-06
TILES = 8
PARTS = 2
WINDOW = 4
LANES = 128
VMEM_LIMIT = 36 * 1024 * 1024
BF16 = jnp.bfloat16
F32 = jnp.float32
NT = (((1,), (1,)), ((), ()))
TN = (((0,), (0,)), ((), ()))
SMEM, VMEM, HBM = pltpu.SMEM, pltpu.VMEM, pltpu.HBM
IDLE, LEFT, RIGHT, APPLY = 0, 1, 2, 3


def unpack(own, others, core, env_ref):
    chunks, rows, width = own.shape
    lanes = env_ref.shape[1] // width
    half = env_ref.shape[0] // 2
    for ref, owner in ((own, 1 - core), (others, core)):
        for j in range(chunks):
            r, k = j // lanes, j % lanes
            start = pl.multiple_of(owner * half + rows * r, rows)
            env_ref[pl.ds(start, rows), width * k : width * (k + 1)] = ref[j]


def hand_out(acc, scale, core, kept, given):
    chunks, rows, width = kept.shape
    lanes = acc.shape[1] // width
    half = acc.shape[0] // 2
    for ref, owner in ((given, 1 - core), (kept, core)):
        start = pl.multiple_of(owner * half, half)
        for j in range(chunks):
            r, k = j // lanes, j % lanes
            value = acc[pl.ds(start + rows * r, rows), width * k : width * (k + 1)]
            if scale is not None:
                value = value * scale
            ref[j] = value.astype(BF16)


def scale_of(*parts):
    wide = [part.astype(F32) for part in parts]
    return lax.rsqrt(sum(jnp.mean(value * value) for value in wide) / len(parts) + EPSILON)


def tile_copies(x_ref, x_buf, sems):
    return [tile_copy(x_ref, x_buf, sems, t) for t in range(TILES)]


def tile_copy(x_ref, x_buf, sems, t):
    rows = x_buf.shape[0] // TILES
    part = block_of(t, rows)
    return pltpu.make_async_copy(x_ref.at[part], x_buf.at[part], sems.at[t])


def block_of(t, size):
    return pl.ds(t * size if isinstance(t, int) else pl.multiple_of(t * size, size), size)


def begin(copies):
    for copy in copies:
        copy.start()


def mode_major(y_buf, y2, points):
    step = y2.shape[0] // TILES

    @pl.loop(0, TILES)
    def _(t):
        y2[block_of(t, step), :] = y_buf[block_of(t, step * points), :].reshape(step, y2.shape[1])


def left_sum(env, x_ref, x, sems, y2, w, acc):
    width = env.shape[0]
    turned = env.T

    @pl.loop(0, y2.shape[1] // (2 * width))
    def _(i):
        lanes = block_of(i, 2 * width)
        w[:, lanes] = jnp.dot(turned, y2[:, lanes], preferred_element_type=F32).astype(BF16)

    rows = x.shape[0] // PARTS
    ranks = w.shape[0] // PARTS

    def term(t):
        for tile in range(TILES // PARTS):
            tile_copy(x_ref, x, sems, t * (TILES // PARTS) + tile).wait()
        own = w[block_of(t, ranks), :].reshape(rows, width)
        return lax.dot_general(own, x[block_of(t, rows), :], TN, preferred_element_type=F32)

    acc[...] = jnp.zeros_like(acc)

    @pl.loop(0, PARTS)
    def _(t):
        acc[...] += term(t)


def carry_back(env, window, x_ref, x, sems, natural, cb, cb_out, store_sems):
    rows = x.shape[0] // TILES
    ranks = cb.shape[0] // TILES
    turned = env.T

    @pl.loop(0, TILES // 2)
    def _(pair):
        for u in range(2):
            t = pair * 2 + u
            tile_copy(x_ref, x, sems, t).wait()
            if window < TILES:

                @pl.when(t + window < TILES)
                def _():
                    tile_copy(x_ref, x, sems, t + window).start()

        for u in range(2):
            value = jnp.dot(x[block_of(pair * 2 + u, rows), :], turned, preferred_element_type=F32)
            natural[u] = value.astype(BF16)
            cb[block_of(pair * 2 + u, ranks), :] = natural[u].reshape(ranks, cb.shape[1])
        for u in range(2):
            tile_copy(cb, cb_out, store_sems, pair * 2 + u).start()


def right_sum(y2, cb, acc):
    half = cb.shape[0] // 2

    @pl.loop(0, 2)
    def _(n):
        acc[:, block_of(n, half)] = lax.dot_general(
            y2[...], cb[block_of(n, half), :], NT, preferred_element_type=F32
        )


def apply(env, x_ref, x, sems, xt, narrow, applied):
    source_rank = env.shape[1]
    rows = x.shape[0] // TILES
    ranks = xt.shape[0] // TILES

    @pl.loop(0, TILES)
    def _(t):
        tile_copy(x_ref, x, sems, t).wait()
        xt[block_of(t, ranks), :] = x[block_of(t, rows), :].reshape(ranks, xt.shape[1])

    @pl.loop(0, xt.shape[1] // source_rank)
    def _(i):
        lanes = block_of(i, source_rank)
        narrow[:, lanes] = jnp.dot(env, xt[:, lanes], preferred_element_type=F32).astype(BF16)

    blocks = applied.shape[1] // source_rank
    own = env.shape[0] // blocks

    @pl.loop(0, blocks)
    def _(j):
        applied[:, block_of(j, source_rank)] = narrow[block_of(j, own), :].reshape(source_rank, source_rank)


def first_kernel(
    points, role, lb, rb, x, y, kept, given, cb_out, y2, x_buf, y_buf, cb, w, natural, acc, env_buf, sems, store_sems, side
):
    load_y = pltpu.make_async_copy(y, y_buf, side.at[0])
    stores = tile_copies(cb, cb_out, store_sems)
    copies = tile_copies(x, x_buf, sems)

    @pl.when(role[0] == IDLE)
    def _():
        load_y.start()
        load_y.wait()
        mode_major(y_buf, y2, points)
        kept[...] = jnp.zeros_like(kept)
        given[...] = jnp.zeros_like(given)

    @pl.when(role[0] == LEFT)
    def _():
        load_y.start()
        load_env = pltpu.make_async_copy(lb, env_buf, side.at[2])
        load_env.start()
        load_y.wait()
        begin(copies)
        mode_major(y_buf, y2, points)
        load_env.wait()
        left_sum(env_buf[...], x, x_buf, sems, y2, w, acc)
        hand_out(acc, None, role[1], kept, given)

    @pl.when(role[0] == RIGHT)
    def _():
        load_env = pltpu.make_async_copy(rb, env_buf, side.at[2])
        load_env.start()
        load_y.start()
        begin(copies[:WINDOW])
        load_env.wait()
        carry_back(env_buf[...], WINDOW, x, x_buf, sems, natural, cb, cb_out, store_sems)
        load_y.wait()
        mode_major(y_buf, y2, points)
        right_sum(y2, cb, acc)
        hand_out(acc, None, role[1], kept, given)
        for store in stores:
            store.wait()


def next_kernel(
    role, e, f, lb, x, y2, kept, given, cb_out, x_buf, cb, w, natural, xt, narrow, acc, env_buf, sems, store_sems, side
):
    stores = tile_copies(cb, cb_out, store_sems)
    copies = tile_copies(x, x_buf, sems)

    @pl.when(role[0] == IDLE)
    def _():
        kept[...] = jnp.zeros_like(kept)
        given[...] = jnp.zeros_like(given)

    @pl.when(role[0] == APPLY)
    def _():
        kept[...] = jnp.zeros_like(kept)
        given[...] = jnp.zeros_like(given)
        load_env = pltpu.make_async_copy(lb, env_buf, side.at[0])
        load_env.start()
        begin(copies)
        load_env.wait()
        apply(env_buf[...], x, x_buf, sems, xt, narrow, cb)
        for store in stores:
            store.start()
        for store in stores:
            store.wait()

    @pl.when(role[0] == LEFT)
    def _():
        begin(copies)
        unpack(e, f, role[1], env_buf)
        env = env_buf[...]
        left_sum(env, x, x_buf, sems, y2, w, acc)
        hand_out(acc, scale_of(env), role[1], kept, given)

    @pl.when(role[0] == RIGHT)
    def _():
        begin(copies)
        unpack(e, f, role[1], env_buf)
        env = env_buf[...]
        carry_back(env, TILES, x, x_buf, sems, natural, cb, cb_out, store_sems)
        right_sum(y2, cb, acc)
        hand_out(acc, scale_of(env), role[1], kept, given)
        for store in stores:
            store.wait()


def last_kernel(
    role, e1, f1, e2, f2, e3, f3, cb0, cb1, cb2, out, cb, out_buf, narrow, env_buf, factor, sems, side
):
    target_rank, source_rank = env_buf.shape
    block = out_buf.shape[0] // TILES
    lanes = cb.shape[1] // TILES

    def load(source, j):
        part = block_of(j, lanes)
        return pltpu.make_async_copy(source.at[:, part], cb.at[:, part], side.at[j])

    def store(t):
        part = block_of(t, block)
        return pltpu.make_async_copy(out_buf.at[part], out.at[part], sems.at[t])

    for group, source in ((0, cb1), (1, cb2), (2, cb1), (3, cb0)):

        @pl.when(role[0] == group)
        def _():
            for j in range(TILES):
                load(source, j).start()

    for group, e, f in ((1, e1, f1), (2, e2, f2)):

        @pl.when(role[0] == group)
        def _():
            unpack(e, f, role[1], env_buf)

    @pl.when((role[0] == 0) | (role[0] == 3))
    def _():
        unpack(e3, f3, role[1], env_buf)

    other = jnp.where(role[0] == 1, scale_of(e2[...], f2[...]), scale_of(e1[...], f1[...]))
    inner = (role[0] == 1) | (role[0] == 2)
    env = env_buf[...]
    factor[0] = scale_of(env) * jnp.where(inner, other, 1.0) * (1.0 / math.sqrt(source_rank))

    @pl.when(role[0] == 0)
    def _():
        @pl.loop(0, TILES)
        def _(t):
            load(cb1, t).wait()
            value = lax.dot_general(cb[:, block_of(t, lanes)], env_buf[...], NT, preferred_element_type=F32)
            out_buf[block_of(t, block), :] = (value * factor[0]).astype(BF16)
            store(t).start()

    @pl.when(role[0] != 0)
    def _():
        @pl.loop(0, TILES)
        def _(j):
            load(cb1, j).wait()
            part = block_of(j, lanes)
            value = jnp.dot(env_buf[...], cb[:, part], preferred_element_type=F32)
            narrow[:, part] = (value * factor[0]).astype(BF16)

        @pl.loop(0, TILES)
        def _(t):
            own = narrow[block_of(t, target_rank // TILES), :]
            out_buf[block_of(t, block), :] = own.reshape(block, target_rank)
            store(t).start()

    for t in range(TILES):
        store(t).wait()


def place(kind):
    return pl.BlockSpec(memory_space=kind)


def in_hbm(array):
    return pltpu.with_memory_space_constraint(array, HBM)


def step_calls(points, target_rank, source_rank):
    chunk = (32, target_rank * source_rank // (64 * LANES), LANES)
    rows = source_rank * points
    flat = points * target_rank
    s_shape = jax.ShapeDtypeStruct(chunk, BF16)
    cb_shape = jax.ShapeDtypeStruct((source_rank, flat), BF16)
    y2_shape = jax.ShapeDtypeStruct((target_rank, flat), BF16)
    x_buf = pltpu.VMEM((rows, source_rank), BF16)
    cb = pltpu.VMEM(cb_shape.shape, BF16)
    y_buf = pltpu.VMEM((target_rank * points, target_rank), BF16)
    w = pltpu.VMEM(cb_shape.shape, BF16)
    natural = pltpu.VMEM((2, rows // TILES, target_rank), BF16)
    xt = pltpu.VMEM((source_rank, points * source_rank), BF16)
    wide = pltpu.VMEM((target_rank, points * source_rank), BF16)
    narrow = pltpu.VMEM((target_rank, flat), BF16)
    acc = pltpu.VMEM((target_rank, source_rank), F32)
    env_buf = pltpu.VMEM((target_rank, source_rank), BF16)
    sems = pltpu.SemaphoreType.DMA((TILES,))
    side = pltpu.SemaphoreType.DMA((3,))
    params = pltpu.CompilerParams(vmem_limit_bytes=VMEM_LIMIT)
    first = pl.pallas_call(
        functools.partial(first_kernel, points),
        out_shape=(s_shape, s_shape, HBM(cb_shape.shape, BF16), y2_shape),
        in_specs=[place(SMEM)] + [place(HBM)] * 4,
        out_specs=(place(VMEM), place(VMEM), place(HBM), place(VMEM)),
        scratch_shapes=[x_buf, y_buf, cb, w, natural, acc, env_buf, sems, sems, side],
        compiler_params=params,
        name="first_step",
    )
    following = pl.pallas_call(
        next_kernel,
        out_shape=(s_shape, s_shape, HBM(cb_shape.shape, BF16)),
        in_specs=[place(SMEM), place(VMEM), place(VMEM), place(HBM), place(HBM), place(VMEM)],
        out_specs=(place(VMEM), place(VMEM), place(HBM)),
        scratch_shapes=[x_buf, cb, w, natural, xt, wide, acc, env_buf, sems, sems, side],
        compiler_params=params,
        name="next_step",
    )
    last = pl.pallas_call(
        last_kernel,
        out_shape=jax.ShapeDtypeStruct((target_rank * points, target_rank), BF16),
        in_specs=[place(SMEM)] + [place(VMEM)] * 6 + [place(HBM)] * 3,
        out_specs=place(HBM),
        scratch_shapes=[cb, y_buf, narrow, env_buf, pltpu.SMEM((1,), F32), sems, sems],
        compiler_params=params,
        name="projection",
    )
    return first, following, last


def exchange(kept, given, route):
    chunks, rows, width = kept.shape
    devices = lax.axis_size("mode")
    same_core = [list(range(c, devices, 2)) for c in range(2)]
    neighbour = [(d, d ^ 1) for d in range(devices)]
    taken = lax.ppermute(given, "mode", neighbour)
    chip = (kept.astype(F32) + taken.astype(F32)).astype(BF16)
    mine = lax.all_to_all(chip, "mode", 0, 0, axis_index_groups=same_core, tiled=True)
    summed = jnp.sum(mine.astype(F32), axis=0).astype(BF16)
    hops = [
        (source * devices + d, target * devices + (d ^ 1)) for source, target in route for d in range(devices)
    ]
    summed = lax.ppermute(summed, ("cores", "mode"), hops)
    copies = jnp.broadcast_to(summed[None], (chunks, rows, width))
    whole = lax.all_to_all(copies, "mode", 0, 0, axis_index_groups=same_core, tiled=True)
    return whole, lax.ppermute(whole, "mode", neighbour)


def body(x_cores, y_cores, left_boundary, right_boundary):
    _, source_rank, points, _ = x_cores.shape
    target_rank = left_boundary.shape[0]
    group = lax.axis_index("cores")
    core = lax.axis_index("mode") % 2
    x = in_hbm(x_cores.reshape(source_rank * points, source_rank))
    y = in_hbm(y_cores.reshape(target_rank * points, target_rank))
    left_boundary, right_boundary = in_hbm(left_boundary), in_hbm(right_boundary)
    first, following, last = step_calls(points, target_rank, source_rank)

    def role_at(position):
        role = jnp.where(group == position, LEFT, jnp.where(group == 3 - position, RIGHT, IDLE))
        if position == 1:
            role = jnp.where(group == 0, APPLY, role)
        return jnp.stack([role, core]).astype(jnp.int32)

    kept, given, cb, y2 = first(role_at(0), left_boundary, right_boundary, x, y)
    carried = [cb]
    envs = [exchange(kept, given, [(0, 1), (3, 2)])]
    for position, route in ((1, [(1, 2), (2, 1)]), (2, [(2, 3), (1, 0)])):
        kept, given, cb = following(role_at(position), *envs[-1], left_boundary, x, y2)
        carried.append(cb)
        envs.append(exchange(kept, given, route))
    out = last(jnp.stack([group, core]).astype(jnp.int32), *sum(envs, ()), *map(in_hbm, carried))
    return out.reshape(1, target_rank, points, target_rank)


def solution(mesh):
    in_specs = (P("cores", None, "mode", None), P("cores", None, "mode", None), P(), P())
    out_specs = P("cores", None, "mode", None)
    return jax.shard_map(body, mesh=mesh, in_specs=in_specs, out_specs=out_specs, check_vma=False)
```
